256 devices in a mesh: ctx: 64 (over x, z, core), tp: 4 (over y).
Axes of the slice: x: 4, y: 4, z: 8, core: 2. Of those that a mesh axis runs over, the one named last changes fastest.
Arguments:
- queries: bfloat16 [32768, 4096], P('ctx', 'tp'), may hold values from -6 to 6
- keys: bfloat16 [32768, 1024], P('ctx', 'tp'), may hold values from -6 to 6
- values: bfloat16 [32768, 1024], P('ctx', 'tp'), may hold values from -6 to 6
- kept_rows: int32 [64, 8, 64], P('ctx', 'tp'), may hold values from 0 to 511, as said below
- out_weight: bfloat16 [4096, 4096], P('tp', 'ctx'), may hold values from -0.5 to 0.5
Outputs:
- mixed: bfloat16 [32768, 4096], P('ctx', 'tp')
The draws below stay inside these ranges and needn't reach their ends.
Inputs may be any that keep to these rules, and one draw needn't show every extreme that they name: `kept_rows`: within each block and key and value head the rows are distinct and rising.
All inputs are finite; a program needn't handle non-finite values.
Results may differ from the reference program's by a relative error of at most 0.017.
Values may be sent and summed in bfloat16 or wider, within the bound.
No kernel may reach another device: no remote copies, remote signals or barrier semaphores. Data moves between devices by JAX's collectives and lax.ppermute only.
A program may use at most 128 MiB of HBM per device.

```python
import jax
import jax.numpy as jnp
from jax import lax

HEADS = 32
KV_HEADS = 8
DH = 128
D = 4096
BLK = 512
KEEP = 64
TOKENS = 32768
N_CTX = 64


def draw_queries(key, part):
    key = jax.random.fold_in(key, 12)
    first = jax.random.fold_in(key, 0)
    shape = (TOKENS, KV_HEADS, HEADS // KV_HEADS, DH)
    base = jnp.clip(jax.random.normal(first, shape, jnp.float32), -6.0, 6.0)
    return base.reshape(TOKENS, HEADS * DH).astype(jnp.bfloat16)


def draw_keys(key, part):
    key = jax.random.fold_in(key, 11)
    shape = (TOKENS, KV_HEADS, DH)
    base = jnp.clip(jax.random.normal(key, shape, jnp.float32), -6.0, 6.0)
    return base.reshape(TOKENS, KV_HEADS * DH).astype(jnp.bfloat16)


def draw_kept_rows(key, part):
    key = jax.random.fold_in(key, 13)
    blocks = TOKENS // BLK
    row_keys = jax.random.split(key, blocks * KV_HEADS)
    indices = jnp.arange(blocks * KV_HEADS, dtype=jnp.int32)

    def one_row(row_key, index):
        first_key, second_key = jax.random.split(row_key)
        middle = jax.random.permutation(first_key, BLK - 2).astype(jnp.int32) + 1
        ends = jnp.array([0, BLK - 1], dtype=jnp.int32)
        anchored = jnp.concatenate([ends, middle[:KEEP - 2]])
        loose = jax.random.permutation(second_key, BLK).astype(jnp.int32)[:KEEP]
        chosen = jnp.where(index == 0, anchored, loose)
        return jnp.sort(chosen)
    return jax.vmap(one_row)(row_keys, indices).reshape(blocks, KV_HEADS, KEEP)


def levels(own_key, dims, cuts, low, high):
    def one(axis_at, parts):
        heights = jax.random.uniform(jax.random.fold_in(jax.random.fold_in(own_key, 6), axis_at), (parts,), jnp.float32, low / len(cuts), high / len(cuts))
        return jnp.repeat(jnp.exp(heights), dims[axis_at] // parts).reshape((-1,) + (1,) * (len(dims) - axis_at - 1))

    loudness = one(*cuts[0])
    for cut in cuts[1:]:
        loudness = loudness * one(*cut)
    return loudness


def bell_draw(stream_key, extent, scale, limit, pieces=(), kind=jnp.bfloat16):
    gain = levels(stream_key, extent, pieces, -0.22, 0.18) if pieces else 1.0
    values = jax.random.normal(stream_key, extent, jnp.float32) * scale * gain
    return jnp.minimum(jnp.maximum(values, -limit), limit).astype(kind)


def setup_inputs(seed: int = 0) -> dict:
    key_of = jax.random.split(jax.random.key(seed), 6)
    return {
        "queries": draw_queries(jax.random.fold_in(key_of[5], 71), 0),
        "keys": draw_keys(jax.random.fold_in(key_of[5], 71), 0),
        "values": bell_draw(key_of[2], (TOKENS, KV_HEADS * DH), 1.0, 6.0, ((0, 64), (1, 4))),
        "kept_rows": draw_kept_rows(jax.random.fold_in(key_of[5], 71), 0),
        "out_weight": bell_draw(key_of[4], (HEADS * DH, D), DH ** -0.5, 0.5, ((0, 4), (1, 64))),
    }


def reference(queries, keys, values, kept_rows, out_weight):
    group_size = HEADS // KV_HEADS
    q_all = queries.reshape(N_CTX, BLK, KV_HEADS, group_size, DH)
    k_all = keys.reshape(N_CTX, BLK, KV_HEADS, DH).transpose(0, 2, 1, 3)
    v_all = values.reshape(N_CTX, BLK, KV_HEADS, DH).transpose(0, 2, 1, 3)
    picks = jnp.broadcast_to(kept_rows[..., None], (N_CTX, KV_HEADS, KEEP, DH))
    kept_k = jnp.take_along_axis(k_all, picks, axis=2).transpose(1, 0, 2, 3).reshape(KV_HEADS, N_CTX * KEEP, DH)
    kept_v = jnp.take_along_axis(v_all, picks, axis=2).transpose(1, 0, 2, 3).reshape(KV_HEADS, N_CTX * KEEP, DH)
    row_pos = jnp.arange(BLK, dtype=jnp.int32)
    slot = jnp.arange(N_CTX * KEEP, dtype=jnp.int32) // KEEP

    def one_block(index):
        q_blk = lax.dynamic_index_in_dim(q_all, index, 0, keepdims=False).transpose(1, 2, 0, 3).astype(jnp.float32)
        k_own = lax.dynamic_index_in_dim(k_all, index, 0, keepdims=False)
        v_own = lax.dynamic_index_in_dim(v_all, index, 0, keepdims=False)
        k_cat = jnp.concatenate([k_own, k_all[0], kept_k], axis=1).astype(jnp.float32)
        v_cat = jnp.concatenate([v_own, v_all[0], kept_v], axis=1).astype(jnp.float32)
        scores = jnp.einsum("hgqd,hkd->hgqk", q_blk, k_cat) * (DH ** -0.5)
        own_ok = row_pos[:, None] >= row_pos[None, :]
        anchor_ok = jnp.broadcast_to(index > 0, (BLK, BLK))
        pass_ok = jnp.broadcast_to(((slot >= 1) & (slot < index))[None, :], (BLK, N_CTX * KEEP))
        allowed = jnp.concatenate([own_ok, anchor_ok, pass_ok], axis=1)
        scores = jnp.where(allowed, scores, -jnp.inf)
        top = jnp.max(scores, axis=-1, keepdims=True)
        weights = jnp.exp(scores - top)
        total = jnp.sum(weights, axis=-1, keepdims=True)
        rounded = lax.optimization_barrier(weights.astype(jnp.bfloat16)).astype(jnp.float32)
        result = jnp.einsum("hgqk,hkd->hgqd", rounded, v_cat) / total
        return result.transpose(2, 0, 1, 3).reshape(BLK, HEADS * DH).astype(jnp.bfloat16)

    attended = lax.map(one_block, jnp.arange(N_CTX, dtype=jnp.int32)).reshape(TOKENS, HEADS * DH)
    return jnp.dot(attended, out_weight, preferred_element_type=jnp.float32).astype(jnp.bfloat16)
```

```python
import functools

import jax
import jax.numpy as jnp
import numpy as np
from jax import lax
from jax.experimental import pallas as pl
from jax.experimental.pallas import tpu as pltpu
from jax.sharding import PartitionSpec as P

DH = 128
BLK = 512
KEEP = 64
GROUP = 4
NX, NZ = 4, 8
SCALE = float(DH**-0.5 * np.log2(np.e))
MASKED = -1e30
LOW, HIGH = 1e-20, 1e30
BF, F32 = jnp.bfloat16, jnp.float32
VMEM = pl.BlockSpec(memory_space=pltpu.VMEM)
SMEM = pl.BlockSpec(memory_space=pltpu.SMEM)


def ctx_id(x, z, core):
    return (x % NX) * 16 + (z % NZ) * 2 + core % 2


def ctx_perm(move, keep=lambda x, z, core: True):
    places = [(x, z, core) for x in range(NX) for z in range(NZ) for core in range(2)]
    return [(ctx_id(*at), ctx_id(*move(*at))) for at in places if keep(*at)]


def x_shift(step):
    return ctx_perm(lambda x, z, core: (x + step, z, core))


def z_shift(step):
    return ctx_perm(lambda x, z, core: (x, z + step, core))


CORE_SWAP = ctx_perm(lambda x, z, core: (x, z, core + 1))


def over_ctx(block, pairs):
    return lax.ppermute(block, "ctx", pairs)


def over_tp(block, step):
    return lax.ppermute(block, "tp", [(y, (y + step) % 4) for y in range(4)])


def prep_kernel(rows_ref, k_ref, v_ref, w_ref, kept_ref, wt_ref):
    col = lax.broadcasted_iota(jnp.int32, (KEEP, BLK), 1)
    for head in range(2):
        pick = jnp.where(rows_ref[head] == col, 1.0, 0.0).astype(BF)
        lanes = slice(head * DH, (head + 1) * DH)
        kept_ref[head] = jnp.dot(pick, k_ref[:, lanes], preferred_element_type=F32).astype(BF)
        kept_ref[2 + head] = jnp.dot(pick, v_ref[:, lanes], preferred_element_type=F32).astype(BF)
    wt_ref[...] = w_ref[...].T


def scores_of(q, k):
    return lax.dot_general(q, k, (((1,), (1,)), ((), ())), preferred_element_type=F32) * SCALE


def lane_sum(p):
    total = p[:, :DH]
    for at in range(DH, p.shape[1], DH):
        total = total + p[:, at : at + DH]
    return total


def attend_kernel(chunks, flag_ref, bias_ref, q_ref, k_ref, v_ref, *refs):
    pieces = refs[: 2 * chunks]
    out_ref, qs, kv, acc, tot, top = refs[2 * chunks :]
    for h in range(8):
        qs[h] = q_ref[:, h * DH : (h + 1) * DH]
    for i in range(chunks):
        for half in range(2):
            for a in range(4):
                for b in range(4):
                    at = (half * 4 + b) * KEEP
                    kv[i, a, at : at + KEEP, :] = pieces[2 * i + half][b, a]
    row = lax.broadcasted_iota(jnp.int32, (BLK, BLK), 0)
    col = lax.broadcasted_iota(jnp.int32, (BLK, BLK), 1)

    def sweep(shifted):
        for head in range(2):
            lanes = slice(head * DH, (head + 1) * DH)
            for g in range(GROUP):
                h = head * GROUP + g
                s = jnp.where(row >= col, scores_of(qs[h], k_ref[:, lanes]), MASKED)
                if shifted:
                    s = s - top[h]
                p = jnp.exp2(s)
                tot[h] = lane_sum(p)
                acc[h] = jnp.dot(p.astype(BF), v_ref[:, lanes], preferred_element_type=F32)

            def step(i, carry):
                @pl.when(flag_ref[i] > 0)
                def _():
                    k, v = kv[i, head], kv[i, 2 + head]
                    bias = bias_ref[i]
                    for g in range(GROUP):
                        h = head * GROUP + g
                        s = scores_of(qs[h], k) + bias
                        if shifted:
                            s = s - top[h]
                        p = jnp.exp2(s)
                        tot[h] += lane_sum(p)
                        acc[h] += jnp.dot(p.astype(BF), v, preferred_element_type=F32)

                return carry

            lax.fori_loop(0, chunks, step, 0)

    def find_top():
        for head in range(2):
            lanes = slice(head * DH, (head + 1) * DH)
            for g in range(GROUP):
                h = head * GROUP + g
                s = jnp.where(row >= col, scores_of(qs[h], k_ref[:, lanes]), MASKED)
                top[h] = jnp.max(s, 1, keepdims=True)

            def step(i, carry):
                @pl.when(flag_ref[i] > 0)
                def _():
                    for g in range(GROUP):
                        h = head * GROUP + g
                        s = scores_of(qs[h], kv[i, head]) + bias_ref[i]
                        top[h] = jnp.maximum(top[h], jnp.max(s, 1, keepdims=True))

                return carry

            lax.fori_loop(0, chunks, step, 0)

    sweep(False)
    sums = [jnp.sum(tot[h], 1, keepdims=True) for h in range(8)]
    least = functools.reduce(jnp.minimum, sums)
    most = functools.reduce(jnp.maximum, sums)
    safe = (jnp.min(least) > LOW) & (jnp.max(most) < HIGH)

    @pl.when(jnp.logical_not(safe))
    def _():
        find_top()
        sweep(True)

    for h in range(8):
        total = jnp.sum(tot[h], 1, keepdims=True)
        out_ref[:, h * DH : (h + 1) * DH] = (acc[h] / total).astype(BF)


def per_device(queries, keys, values, kept_rows, out_weight):
    ctx, tp = lax.axis_index("ctx"), lax.axis_index("tp")
    x, z, core = ctx // 16, (ctx // 2) % NZ, ctx % 2

    kept, wt = pl.pallas_call(
        prep_kernel,
        out_shape=(
            jax.ShapeDtypeStruct((4, KEEP, DH), BF),
            jax.ShapeDtypeStruct((64, 1024), BF),
        ),
        in_specs=[VMEM] * 4,
        out_specs=(VMEM, VMEM),
        name="prep",
    )(kept_rows.reshape(2, KEEP, 1), keys, values, out_weight)

    swap = [
        (ctx_id(a, zz, cc) * 4 + b, ctx_id(b, zz, cc) * 4 + a)
        for a in range(4)
        for b in range(4)
        for zz in range(NZ)
        for cc in range(2)
    ]
    wt = lax.ppermute(wt, ("ctx", "tp"), swap)
    wall = lax.all_gather(wt, "ctx", axis=0, tiled=True).reshape(4, 1024, 1024)

    def along_x(block):
        return jnp.stack([block] + [over_ctx(block, x_shift(d)) for d in (1, 2, 3)])

    first = along_x(kept)
    near = {0: first}
    up, down = first, first
    for r in (1, 2, 3):
        up, down = over_ctx(up, z_shift(1)), over_ctx(down, z_shift(-1))
        near[r], near[NZ - r] = up, down
    near[4] = jnp.concatenate(
        [over_ctx(up[:2], z_shift(1)), over_ctx(down[2:], z_shift(-1))]
    )

    own = jnp.concatenate(
        [keys.reshape(BLK, 2, DH).transpose(1, 0, 2), values.reshape(BLK, 2, DH).transpose(1, 0, 2)]
    ).reshape(4, 4, 2, KEEP, DH)
    here = own[:, :, 0]
    other = over_ctx(own[:, :, 1], [(0, 1)])
    mine = jnp.where(core == 0, here, other)
    root = (x == 0) & (z == 0)
    piece = jnp.where(root, mine[:, 0], jnp.zeros_like(mine[:, 0]))
    for d in (1, 2, 3):
        piece = piece + over_ctx(
            mine[:, d], [(ctx_id(0, 0, cc), ctx_id(d, 0, cc)) for cc in range(2)]
        )
    for hop, starts in ((4, (0,)), (2, (0, 4)), (1, (0, 2, 4, 6))):
        pairs = ctx_perm(lambda a, b, cc: (a, b + hop, cc), lambda a, b, cc: b in starts)
        piece = piece + over_ctx(piece, pairs)
    anchor = along_x(piece)

    parts = [anchor] + [near[d] for d in range(NZ)]
    pairs = []
    for part in parts:
        pairs += [part, over_ctx(part, CORE_SWAP)]
    chunks = len(parts)

    zs = ((z - jnp.arange(NZ)) % NZ)[:, None, None]
    cs = ((core + jnp.arange(2)) % 2)[None, :, None]
    xs = ((x - jnp.arange(NX)) % NX)[None, None, :]
    block = xs * 16 + zs * 2 + cs
    seen = ((block >= 1) & (block < ctx)).reshape(NZ, 8)
    seen = jnp.concatenate([jnp.broadcast_to(ctx > 0, (1, 8)), seen])
    flags = jnp.any(seen, 1).astype(jnp.int32)
    bias = jnp.repeat(jnp.where(seen, 0.0, MASKED).astype(F32), KEEP, axis=1).reshape(chunks, 1, BLK)

    attended = pl.pallas_call(
        functools.partial(attend_kernel, chunks),
        out_shape=jax.ShapeDtypeStruct((BLK, 1024), BF),
        in_specs=[SMEM] + [VMEM] * (4 + 2 * chunks),
        out_specs=VMEM,
        scratch_shapes=[
            pltpu.VMEM((8, BLK, DH), BF),
            pltpu.VMEM((chunks, 4, BLK, DH), BF),
            pltpu.VMEM((8, BLK, DH), F32),
            pltpu.VMEM((8, BLK, DH), F32),
            pltpu.VMEM((8, BLK, 1), F32),
        ],
        compiler_params=pltpu.CompilerParams(vmem_limit_bytes=48 * 2**20),
        cost_estimate=pl.CostEstimate(flops=2 * 10**10, bytes_accessed=8 * 2**20, transcendentals=0),
        name="attend",
    )(flags, bias, queries, keys, values, *pairs)

    def project(block, step, lo, hi):
        weight = lax.dynamic_index_in_dim(wall, (tp + step) % 4, 0, keepdims=False)[:, lo:hi]
        return lax.dot_general(block, weight, (((1,), (1,)), ((), ())), preferred_element_type=F32)

    left, right = over_tp(attended, 1), over_tp(attended, -1)
    far_l, far_r = over_tp(left[:, :512], 1), over_tp(right[:, 512:], -1)
    out = project(attended, 0, 0, 1024) + project(left, 3, 0, 1024) + project(right, 1, 0, 1024)
    out = out + project(far_l, 2, 0, 512) + project(far_r, 2, 512, 1024)
    return out.astype(BF)


def solution(mesh):
    placed = (P("ctx", "tp"), P("ctx", "tp"), P("ctx", "tp"), P("ctx", "tp", None), P("tp", "ctx"))
    return jax.shard_map(
        per_device, mesh=mesh, in_specs=placed, out_specs=P("ctx", "tp"), check_vma=False
    )
```

```python
import functools

import jax
import jax.numpy as jnp
import numpy as np
from jax import lax
from jax.experimental import pallas as pl
from jax.experimental.pallas import tpu as pltpu
from jax.sharding import PartitionSpec as P

DH = 128
BLK = 512
KEEP = 64
GROUP = 4
NX, NZ = 4, 8
ORDER = (0, 1, 2, 3, 4, 6, 5, 7)
UNITS, HEAD = 9, 5
SCALE = float(DH**-0.5 * np.log2(np.e))
MASKED = -1e30
LOW, HIGH = 1e-20, 1e30
BF, F32 = jnp.bfloat16, jnp.float32
VMEM = pl.BlockSpec(memory_space=pltpu.VMEM)
SMEM = pl.BlockSpec(memory_space=pltpu.SMEM)
ANY = pl.BlockSpec(memory_space=pl.ANY)
HBM = pl.BlockSpec(memory_space=pltpu.HBM)
STATE = jax.ShapeDtypeStruct((2, GROUP, BLK, DH), F32)
NT = (((1,), (1,)), ((), ()))


def ctx_id(x, z, core):
    return (x % NX) * 16 + (z % NZ) * 2 + core % 2


def ctx_perm(move, keep=lambda x, z, core: True):
    places = [(x, z, core) for x in range(NX) for z in range(NZ) for core in range(2)]
    return [(ctx_id(*at), ctx_id(*move(*at))) for at in places if keep(*at)]


def along_x(block, step):
    return lax.ppermute(block, "ctx", ctx_perm(lambda x, z, core: (x + step, z, core)))


def along_z(block, step):
    return lax.ppermute(block, "ctx", ctx_perm(lambda x, z, core: (x, z + step, core)))


def to_core(block):
    return lax.ppermute(block, "ctx", ctx_perm(lambda x, z, core: (x, z, core + 1)))


def over_tp(block, step):
    return lax.ppermute(block, "tp", [(y, (y + step) % 4) for y in range(4)])


def call(kernel, name, pieces=0, vmem=12, **kw):
    cost = pl.CostEstimate(flops=int(5e8 + 2.4e9 * pieces), bytes_accessed=2**20, transcendentals=0)
    params = pltpu.CompilerParams(vmem_limit_bytes=vmem * 2**20)
    return pl.pallas_call(kernel, name=name, cost_estimate=cost, compiler_params=params, **kw)


def prep_kernel(core_ref, rows_ref, q_ref, k_ref, v_ref, *refs):
    mine_ref, send_ref, kept_ref, kept_send_ref, first_ref, first_send_ref = refs
    row = lax.broadcasted_iota(jnp.int32, (BLK, KEEP), 0)
    core = core_ref[0]
    for head, out, kept, first in (
        (core, mine_ref, kept_ref, first_ref),
        (1 - core, send_ref, kept_send_ref, first_send_ref),
    ):
        lanes = pl.ds(pl.multiple_of(head * DH, DH), DH)
        pick = jnp.where(rows_ref[pl.ds(head, 1), :] == row, 1.0, 0.0).astype(BF)
        for at, ref in enumerate((k_ref, v_ref)):
            block = ref[:, lanes]
            kept[at] = lax.dot_general(
                pick, block, (((0,), (0,)), ((), ())), preferred_element_type=F32
            ).astype(BF)
            out[:, 512 + at * DH : 640 + at * DH] = block
            for quarter in range(4):
                first[quarter, at] = block[quarter * DH : (quarter + 1) * DH]
    for head, out in ((core, mine_ref), (1 - core, send_ref)):
        out[:, :512] = q_ref[:, pl.ds(pl.multiple_of(head * 512, 512), 512)]


def scores_of(q, k):
    return lax.dot_general(q, k, NT, preferred_element_type=F32) * SCALE


def lane_sum(p):
    total = p[:, :DH]
    for at in range(DH, p.shape[1], DH):
        total = total + p[:, at : at + DH]
    return total


def group_lanes(g):
    return slice(g * DH, (g + 1) * DH)


def causal(s):
    row = lax.broadcasted_iota(jnp.int32, (BLK, BLK), 0)
    col = lax.broadcasted_iota(jnp.int32, (BLK, BLK), 1)
    return jnp.where(row >= col, s, MASKED)


def own_kernel(other_ref, mine_ref, q_ref, acc, tot):
    q_ref[0] = other_ref[...]
    q_ref[1] = mine_ref[...]

    def side_step(side, carry):
        for g in range(GROUP):
            p = jnp.exp2(causal(scores_of(q_ref[side, :, group_lanes(g)], q_ref[side, :, 512:640])))
            tot[side, g] = lane_sum(p)
            acc[side, g] = jnp.dot(p.astype(BF), q_ref[side, :, 640:], preferred_element_type=F32)
        return carry

    lax.fori_loop(0, 2, side_step, 0)


def keys_of(piece):
    rows = piece.shape[0] * DH
    return piece[:, 0].reshape(rows, DH), piece[:, 1].reshape(rows, DH)


def absorb(q_ref, piece_ref, flag, bias, acc, tot):
    @pl.when(flag > 0)
    def _():
        k, v = keys_of(piece_ref)
        for g in range(GROUP):
            p = jnp.exp2(scores_of(q_ref[:, group_lanes(g)], k) + bias)
            tot[g] += lane_sum(p)
            acc[g] += jnp.dot(p.astype(BF), v, preferred_element_type=F32)


def both_kernel(at, flag_ref, bias_ref, q_ref, piece, _acc, _tot, acc, tot):
    def side_step(side, carry):
        absorb(q_ref.at[side], piece, flag_ref[side, at], bias_ref[side, at], acc.at[side], tot.at[side])
        return carry

    lax.fori_loop(0, 2, side_step, 0)


def absorb_all(side, parts, flag_ref, bias_ref, q_ref, pieces, acc, tot):
    for (at, lo, hi), piece in zip(parts, pieces):
        bias = bias_ref[side, at, :, lo * DH : hi * DH]
        absorb(q_ref, piece, flag_ref[side, at], bias, acc, tot)


def side_kernel(side, parts, flag_ref, bias_ref, both_ref, acc_in, tot_in, *refs):
    pieces, (acc, tot) = refs[: len(parts)], refs[len(parts) :]
    acc[...] = acc_in[side]
    tot[...] = tot_in[side]
    absorb_all(side, parts, flag_ref, bias_ref, both_ref.at[side], pieces, acc, tot)


def last_kernel(side, parts, flag_ref, bias_ref, both_ref, acc_in, tot_in, *refs):
    pieces, refs = refs[: len(parts)], refs[len(parts) :]
    everything, (out_ref, acc, tot, kv, top, sems) = refs[:5], refs[5:]
    q_ref = both_ref.at[side]
    acc[...] = acc_in[side] if len(acc_in.shape) == 4 else acc_in[...]
    tot[...] = tot_in[side] if len(tot_in.shape) == 4 else tot_in[...]
    absorb_all(side, parts, flag_ref, bias_ref, q_ref, pieces, acc, tot)
    sums = [jnp.sum(tot[g], 1, keepdims=True) for g in range(GROUP)]
    least = jnp.min(functools.reduce(jnp.minimum, sums))
    most = jnp.max(functools.reduce(jnp.maximum, sums))

    @pl.when(jnp.logical_not((least > LOW) & (most < HIGH)))
    def _():
        places = [kv.at[0], kv.at[1], kv.at[2, :HEAD], kv.at[2, HEAD:], kv.at[3]]
        copies = [
            pltpu.make_async_copy(ref, place, sems.at[i])
            for i, (ref, place) in enumerate(zip(everything, places))
        ]
        for copy in copies:
            copy.start()
        for copy in copies:
            copy.wait()

        def one_group(g, carry):
            q = q_ref[:, pl.ds(pl.multiple_of(g * DH, DH), DH)]
            s = causal(scores_of(q, q_ref[:, 512:640]))
            peak = jnp.max(s, 1, keepdims=True)
            p = jnp.exp2(s - peak)
            top[...] = peak
            tot[g] = lane_sum(p)
            acc[g] = jnp.dot(p.astype(BF), q_ref[:, 640:], preferred_element_type=F32)

            def one_piece(i, carry):
                @pl.when(flag_ref[side, i] > 0)
                def _():
                    k, v = keys_of(kv.at[i])
                    s = scores_of(q, k) + bias_ref[side, i]
                    old = top[...]
                    peak = jnp.maximum(old, jnp.max(s, 1, keepdims=True))
                    fade = jnp.exp2(old - peak)
                    p = jnp.exp2(s - peak)
                    top[...] = peak
                    tot[g] = tot[g] * fade + lane_sum(p)
                    acc[g] = acc[g] * fade + jnp.dot(p.astype(BF), v, preferred_element_type=F32)

                return carry

            return lax.fori_loop(0, NX, one_piece, carry)

        lax.fori_loop(0, GROUP, one_group, 0)

    for g in range(GROUP):
        total = jnp.sum(tot[g], 1, keepdims=True)
        out_ref[:, group_lanes(g)] = (acc[g] / total).astype(BF)


def after(block, *others):
    return lax.optimization_barrier((block,) + others)[0]


def together(*blocks):
    return lax.optimization_barrier(blocks)


def sync(live):
    return dict(zip(live, together(*live.values())))


def per_device(queries, keys, values, kept_rows, out_weight):
    ctx, tp = lax.axis_index("ctx"), lax.axis_index("tp")
    x, z, core = ctx // 16, (ctx // 2) % NZ, ctx % 2

    col = jnp.arange(UNITS * DH)
    back = sum(jnp.where(col // DH == i, d, 0) for i, d in enumerate(ORDER))
    xs = ((x - jnp.arange(NX)) % NX).reshape(1, NX, 1, 1)
    block = xs * 16 + ((z - back) % NZ) * 2 + (core + col // KEEP) % 2
    asking = jnp.stack([ctx + 1 - 2 * core, ctx]).reshape(2, 1, 1, 1)
    seen = jnp.where(col // DH == UNITS - 1, asking > 0, (block >= 1) & (block < asking))
    flags = jnp.any(seen, (2, 3)).astype(jnp.int32)
    bias = jnp.where(seen, 0.0, MASKED).astype(F32)

    wide, kept = jax.ShapeDtypeStruct((BLK, 768), BF), jax.ShapeDtypeStruct((2, KEEP, DH), BF)
    quarters = jax.ShapeDtypeStruct((4, 2, DH, DH), BF)
    mine, send, kept, kept_send, first, first_send = call(
        prep_kernel,
        "prep",
        out_shape=(wide, wide, kept, kept, quarters, quarters),
        in_specs=[SMEM] + [VMEM] * 4,
        out_specs=(VMEM,) * 6,
    )(core.reshape(1), kept_rows.reshape(2, KEEP), queries, keys, values)
    parts_w = []
    for k in range(4):
        pairs = [
            (ctx_id(a, b, c) * 4 + y, ctx_id(y - k, b, c) * 4 + a)
            for a in range(NX)
            for y in range(4)
            for b in range(NZ)
            for c in range(2)
        ]
        parts_w.append(lax.ppermute(out_weight.T, ("ctx", "tp"), pairs))
    live = sync(dict(zip(range(4), parts_w), mine=mine, send=send, kept=kept, kept_send=kept_send,
                     first=first, first_send=first_send, bias=bias))

    parts_w = jnp.stack([live.pop(k) for k in range(4)])
    mine_w = lax.dynamic_slice_in_dim(parts_w, core * 512, 512, 2)
    recv_w = to_core(lax.dynamic_slice_in_dim(parts_w, (1 - core) * 512, 512, 2))
    live["w0"] = jnp.where(
        core == 0, jnp.concatenate([mine_w, recv_w], 1), jnp.concatenate([recv_w, mine_w], 1)
    )
    live["unit"] = jnp.concatenate([live.pop("kept"), to_core(live.pop("kept_send"))], 1)
    first = live["first"]
    first = jnp.where(ctx == 0, first, jnp.zeros_like(first))
    live["first"] = first + lax.ppermute(live.pop("first_send"), "ctx", [(0, 1)])
    live = sync(live)

    unit, first = live["unit"], live["first"]
    live["up"], live["down"] = along_z(unit, 1), along_z(unit, -1)
    opposite = along_z(unit, 4)
    piece = first[0]
    for d in (1, 2, 3):
        pairs = [(ctx_id(0, 0, c), ctx_id(d, 0, c)) for c in range(2)]
        piece = piece + lax.ppermute(first[d], "ctx", pairs)
    live["piece"] = piece
    live["other"] = to_core(live.pop("send"))
    del live["first"]
    live = sync(live)

    def spread(piece, hop):
        return lax.ppermute(piece, "ctx", ctx_perm(lambda a, b, c: (a, b + hop, c), lambda a, b, c: b == 0))

    unit, up, down, piece = live.pop("unit"), live.pop("up"), live.pop("down"), live.pop("piece")
    up2, down2 = together(jnp.stack([unit, up]), jnp.stack([unit, down]))
    up2, down2 = together(along_z(up2, 2), along_z(down2, -2))
    piece = piece + sum(spread(piece, hop) for hop in range(1, NZ))
    live["both"], live["acc"], live["tot"] = call(
        own_kernel,
        "own",
        1,
        out_shape=(jax.ShapeDtypeStruct((2, BLK, 768), BF), STATE, STATE),
        in_specs=[VMEM] * 2,
        out_specs=(VMEM,) * 3,
    )(live.pop("other"), live.pop("mine"))
    live["row"] = jnp.concatenate(
        [jnp.stack([unit, up]), up2, opposite[None], down2, jnp.stack([down, piece])]
    )
    live = sync(live)

    def ring_w(r):
        up, down = live[f"w{r - 1}"], live[f"w{(NZ + 1 - r) % NZ}"]
        if r == 4:
            up, down = along_z(up[:2], 1), along_z(down[2:], -1)
            live["w4"] = jnp.concatenate([up, down])
        else:
            live[f"w{r}"], live[f"w{NZ - r}"] = along_z(up, 1), along_z(down, -1)

    row = live["row"]
    live["left"], live["right"] = along_x(row, 1), along_x(row, -1)
    ring_w(1)
    live["acc"], live["tot"] = call(
        functools.partial(both_kernel, 0),
        "step",
        2,
        out_shape=(STATE,) * 2,
        in_specs=[SMEM] + [VMEM] * 5,
        out_specs=(VMEM,) * 2,
        input_output_aliases={4: 0, 5: 1},
    )(flags, live["bias"], live["both"], row, live["acc"], live["tot"])
    live = sync(live)

    live["far_l"] = along_x(live["left"][:HEAD], 1)
    live["far_r"] = along_x(live["right"][HEAD:], -1)
    ring_w(2)
    behind = {name: live.pop(name) for name in ("w2", "w6")}
    half = jax.ShapeDtypeStruct(STATE.shape[1:], F32)
    near_parts = [(1, 0, UNITS), (3, 0, UNITS)]
    far_parts = [(2, 0, HEAD), (2, HEAD, UNITS)]
    live["acc0"], live["tot0"] = call(
        functools.partial(side_kernel, 0, near_parts),
        "step",
        2,
        out_shape=(half, half),
        in_specs=[SMEM] + [VMEM] * 6,
        out_specs=(VMEM,) * 2,
    )(flags, live["bias"], live["both"], live["acc"], live["tot"], live["left"], live["right"])
    live = sync(live)

    near, far = ("left", "right"), ("far_l", "far_r")

    def last(side, parts, states, pieces):
        names = ("row", "left", "far_l", "far_r", "right")
        return call(
            functools.partial(last_kernel, side, parts),
            "last",
            len(parts) / 2,
            vmem=20,
            out_shape=jax.ShapeDtypeStruct((BLK, 512), BF),
            in_specs=[SMEM] + [VMEM] * (4 + len(parts)) + [ANY] * 5,
            out_specs=VMEM,
            scratch_shapes=[
                pltpu.VMEM(STATE.shape[1:], F32),
                pltpu.VMEM(STATE.shape[1:], F32),
                pltpu.VMEM((NX, UNITS, 2, DH, DH), BF),
                pltpu.VMEM((BLK, 1), F32),
                pltpu.SemaphoreType.DMA((5,)),
            ],
        )(flags, live["bias"], live["both"], *[live[n] for n in states + pieces + names])

    live.update(behind)
    live["a0"] = last(0, far_parts, ("acc0", "tot0"), far)
    del live["acc0"], live["tot0"]
    live = sync(live)

    live["left0"], live["right0"] = over_tp(live["a0"], 1), over_tp(live["a0"], -1)
    ring_w(3)
    live["a1"] = last(1, near_parts + far_parts, ("acc", "tot"), near + far)
    for name in ("acc", "tot", "both", "bias", "row") + near + far:
        del live[name]
    live = sync(live)

    live["left1"], live["right1"] = over_tp(live["a1"], 1), over_tp(live["a1"], -1)
    live["far_l0"] = over_tp(live["left0"][:, :256], 1)
    live["far_r0"] = over_tp(live["right0"][:, 256:], -1)
    ring_w(4)
    live = sync(live)

    weight = jnp.zeros((4, NZ, 128, 512), BF)
    for d in range(NZ):
        weight = lax.dynamic_update_slice(weight, live[f"w{d}"][:, None], (0, (z - d) % NZ, 0, 0))

    def project(block, step, lanes=slice(None)):
        part = lax.dynamic_index_in_dim(weight, (tp + step - x) % 4, 0, keepdims=False)
        part = part.reshape(1024, 512)[:, lanes]
        return lax.dot_general(block, part, NT, preferred_element_type=F32)

    def nearest(a, left, right):
        return project(a, 0) + project(left, 3) + project(right, 1)

    def farthest(far_l, far_r):
        return project(far_l, 2, slice(0, 256)) + project(far_r, 2, slice(256, 512))

    a0, left0, right0 = live["a0"], live["left0"], live["right0"]
    live["far_l1"] = over_tp(live["left1"][:, :256], 1)
    live["far_r1"] = over_tp(live["right1"][:, 256:], -1)
    total = nearest(a0, left0, right0) + farthest(live["far_l0"], live["far_r0"])
    live["total"] = total.astype(BF)
    live["second"] = nearest(live["a1"], live["left1"], live["right1"])
    live["weight"] = weight
    live = sync(live)

    weight = live["weight"]
    total = to_core(live["total"]).astype(F32)
    return (live["second"] + farthest(live["far_l1"], live["far_r1"]) + total).astype(BF)


def solution(mesh):
    placed = (P("ctx", "tp"), P("ctx", "tp"), P("ctx", "tp"), P("ctx", "tp", None), P("tp", "ctx"))
    return jax.shard_map(
        per_device, mesh=mesh, in_specs=placed, out_specs=P("ctx", "tp"), check_vma=False
    )
```

```python
import functools

import jax
import jax.numpy as jnp
import numpy as np
from jax import lax
from jax.experimental import pallas as pl
from jax.experimental.pallas import tpu as pltpu
from jax.sharding import PartitionSpec as P

DH = 128
BLK = 512
KEEP = 64
GROUP = 4
NX, NZ = 4, 8
ORDER = (0, 1, 2, 3, 4, 6, 5, 7)
UNITS, HEAD = 9, 5
SCALE = float(DH**-0.5 * np.log2(np.e))
MASKED = -1e30
LOW, HIGH = 1e-20, 1e30
BF, F32 = jnp.bfloat16, jnp.float32
VMEM = pl.BlockSpec(memory_space=pltpu.VMEM)
SMEM = pl.BlockSpec(memory_space=pltpu.SMEM)
ANY = pl.BlockSpec(memory_space=pl.ANY)
HBM = pl.BlockSpec(memory_space=pltpu.HBM)
STATE = jax.ShapeDtypeStruct((2, GROUP, BLK, DH), F32)
NT = (((1,), (1,)), ((), ()))


def ctx_id(x, z, core):
    return (x % NX) * 16 + (z % NZ) * 2 + core % 2


def ctx_perm(move, keep=lambda x, z, core: True):
    places = [(x, z, core) for x in range(NX) for z in range(NZ) for core in range(2)]
    return [(ctx_id(*at), ctx_id(*move(*at))) for at in places if keep(*at)]


def along_x(block, step):
    return lax.ppermute(block, "ctx", ctx_perm(lambda x, z, core: (x + step, z, core)))


def along_z(block, step):
    return lax.ppermute(block, "ctx", ctx_perm(lambda x, z, core: (x, z + step, core)))


def to_core(block):
    return lax.ppermute(block, "ctx", ctx_perm(lambda x, z, core: (x, z, core + 1)))


def over_tp(block, step):
    return lax.ppermute(block, "tp", [(y, (y + step) % 4) for y in range(4)])


def call(kernel, name, pieces=0, vmem=12, **kw):
    cost = pl.CostEstimate(flops=int(5e8 + 2.4e9 * pieces), bytes_accessed=2**20, transcendentals=0)
    params = pltpu.CompilerParams(vmem_limit_bytes=vmem * 2**20)
    return pl.pallas_call(kernel, name=name, cost_estimate=cost, compiler_params=params, **kw)


def prep_kernel(core_ref, rows_ref, q_ref, k_ref, v_ref, *refs):
    mine_ref, send_ref, kept_ref, kept_send_ref, first_ref, first_send_ref = refs
    row = lax.broadcasted_iota(jnp.int32, (BLK, KEEP), 0)
    core = core_ref[0]
    for head, out, kept, first in (
        (core, mine_ref, kept_ref, first_ref),
        (1 - core, send_ref, kept_send_ref, first_send_ref),
    ):
        lanes = pl.ds(pl.multiple_of(head * DH, DH), DH)
        pick = jnp.where(rows_ref[pl.ds(head, 1), :] == row, 1.0, 0.0).astype(BF)
        for at, ref in enumerate((k_ref, v_ref)):
            block = ref[:, lanes]
            kept[at] = lax.dot_general(
                pick, block, (((0,), (0,)), ((), ())), preferred_element_type=F32
            ).astype(BF)
            out[:, 512 + at * DH : 640 + at * DH] = block
            for quarter in range(4):
                first[quarter, at] = block[quarter * DH : (quarter + 1) * DH]
    for head, out in ((core, mine_ref), (1 - core, send_ref)):
        out[:, :512] = q_ref[:, pl.ds(pl.multiple_of(head * 512, 512), 512)]


def scores_of(q, k):
    return lax.dot_general(q, k, NT, preferred_element_type=F32) * SCALE


def lane_sum(p):
    total = p[:, :DH]
    for at in range(DH, p.shape[1], DH):
        total = total + p[:, at : at + DH]
    return total


def group_lanes(g):
    return slice(g * DH, (g + 1) * DH)


def causal(s):
    row = lax.broadcasted_iota(jnp.int32, (BLK, BLK), 0)
    col = lax.broadcasted_iota(jnp.int32, (BLK, BLK), 1)
    return jnp.where(row >= col, s, MASKED)


def own_kernel(other_ref, mine_ref, q_ref, acc, tot):
    q_ref[0] = other_ref[...]
    q_ref[1] = mine_ref[...]

    def side_step(side, carry):
        for g in range(GROUP):
            p = jnp.exp2(causal(scores_of(q_ref[side, :, group_lanes(g)], q_ref[side, :, 512:640])))
            tot[side, g] = lane_sum(p)
            acc[side, g] = jnp.dot(p.astype(BF), q_ref[side, :, 640:], preferred_element_type=F32)
        return carry

    lax.fori_loop(0, 2, side_step, 0)


def keys_of(piece):
    rows = piece.shape[0] * DH
    return piece[:, 0].reshape(rows, DH), piece[:, 1].reshape(rows, DH)


def absorb(q_ref, piece_ref, flag, bias, acc, tot):
    @pl.when(flag > 0)
    def _():
        k, v = keys_of(piece_ref)
        for g in range(GROUP):
            p = jnp.exp2(scores_of(q_ref[:, group_lanes(g)], k) + bias)
            tot[g] += lane_sum(p)
            acc[g] += jnp.dot(p.astype(BF), v, preferred_element_type=F32)


def both_kernel(at, flag_ref, bias_ref, q_ref, piece, _acc, _tot, acc, tot):
    def side_step(side, carry):
        absorb(q_ref.at[side], piece, flag_ref[side, at], bias_ref[side, at], acc.at[side], tot.at[side])
        return carry

    lax.fori_loop(0, 2, side_step, 0)


def absorb_all(side, parts, flag_ref, bias_ref, q_ref, pieces, acc, tot):
    for (at, lo, hi), piece in zip(parts, pieces):
        bias = bias_ref[side, at, :, lo * DH : hi * DH]
        absorb(q_ref, piece, flag_ref[side, at], bias, acc, tot)


def side_kernel(side, parts, flag_ref, bias_ref, both_ref, acc_in, tot_in, *refs):
    pieces, (acc, tot) = refs[: len(parts)], refs[len(parts) :]
    acc[...] = acc_in[side]
    tot[...] = tot_in[side]
    absorb_all(side, parts, flag_ref, bias_ref, both_ref.at[side], pieces, acc, tot)


def last_kernel(side, parts, flag_ref, bias_ref, both_ref, acc_in, tot_in, *refs):
    pieces, refs = refs[: len(parts)], refs[len(parts) :]
    everything, (out_ref, acc, tot, kv, top, sems) = refs[:5], refs[5:]
    q_ref = both_ref.at[side]
    acc[...] = acc_in[side] if len(acc_in.shape) == 4 else acc_in[...]
    tot[...] = tot_in[side] if len(tot_in.shape) == 4 else tot_in[...]
    absorb_all(side, parts, flag_ref, bias_ref, q_ref, pieces, acc, tot)
    sums = [jnp.sum(tot[g], 1, keepdims=True) for g in range(GROUP)]
    least = jnp.min(functools.reduce(jnp.minimum, sums))
    most = jnp.max(functools.reduce(jnp.maximum, sums))

    @pl.when(jnp.logical_not((least > LOW) & (most < HIGH)))
    def _():
        places = [kv.at[0], kv.at[1], kv.at[2, :HEAD], kv.at[2, HEAD:], kv.at[3]]
        copies = [
            pltpu.make_async_copy(ref, place, sems.at[i])
            for i, (ref, place) in enumerate(zip(everything, places))
        ]
        for copy in copies:
            copy.start()
        for copy in copies:
            copy.wait()

        def one_group(g, carry):
            q = q_ref[:, pl.ds(pl.multiple_of(g * DH, DH), DH)]
            s = causal(scores_of(q, q_ref[:, 512:640]))
            peak = jnp.max(s, 1, keepdims=True)
            p = jnp.exp2(s - peak)
            top[...] = peak
            tot[g] = lane_sum(p)
            acc[g] = jnp.dot(p.astype(BF), q_ref[:, 640:], preferred_element_type=F32)

            def one_piece(i, carry):
                @pl.when(flag_ref[side, i] > 0)
                def _():
                    k, v = keys_of(kv.at[i])
                    s = scores_of(q, k) + bias_ref[side, i]
                    old = top[...]
                    peak = jnp.maximum(old, jnp.max(s, 1, keepdims=True))
                    fade = jnp.exp2(old - peak)
                    p = jnp.exp2(s - peak)
                    top[...] = peak
                    tot[g] = tot[g] * fade + lane_sum(p)
                    acc[g] = acc[g] * fade + jnp.dot(p.astype(BF), v, preferred_element_type=F32)

                return carry

            return lax.fori_loop(0, NX, one_piece, carry)

        lax.fori_loop(0, GROUP, one_group, 0)

    for g in range(GROUP):
        total = jnp.sum(tot[g], 1, keepdims=True)
        out_ref[:, group_lanes(g)] = (acc[g] / total).astype(BF)


def products(blocks, weights, where_ref, slots, group):
    total = None
    for block, (slot, lo, hi) in zip(blocks, slots):
        k = where_ref[slot]
        w = jnp.concatenate([weights[i](k, lo, hi) for i in group])
        term = lax.dot_general(block, w, NT, preferred_element_type=F32)
        total = term if total is None else total + term
    return [total[:, i * DH : (i + 1) * DH] for i in range(len(group))]


def lanes_of(where_ref, i):
    return pl.ds(pl.multiple_of(where_ref[4 + i] * DH, DH), DH)


def piece_of(ref):
    return lambda k, lo, hi: ref[k, :, lo:hi]


NEAR = ((0, 0, 512), (1, 0, 512), (2, 0, 512))
FAR = ((3, 0, 256), (3, 256, 512))


def near_kernel(where_ref, *refs):
    blocks, weights, out_ref = refs[:3], [piece_of(ref) for ref in refs[3:10]], refs[10]
    for group in ((0, 1), (2, 3), (4, 5), (6,)):
        parts = products([ref[...] for ref in blocks], weights, where_ref, NEAR, group)
        for i, part in zip(group, parts):
            out_ref[:, lanes_of(where_ref, i)] = part


def far_kernel(side, where_ref, near_ref, *refs):
    blocks, far, weights, (up, down, out_ref) = refs[:3], refs[3:5], refs[5:12], refs[12:]

    def last_piece(k, lo, hi):
        return jnp.where(k < 2, up[jnp.minimum(k, 1), :, lo:hi], down[jnp.maximum(k - 2, 0), :, lo:hi])

    weights = [piece_of(ref) for ref in weights] + [last_piece]
    for group in ((0, 1), (2, 3), (4, 5), (6, 7)):
        parts = products([ref[side] for ref in far], weights, where_ref, FAR, group)
        for i, part in zip(group, parts):
            lanes = lanes_of(where_ref, i)
            if i == 7:
                near = products([ref[...] for ref in blocks], weights, where_ref, NEAR, (7,))[0]
            else:
                near = near_ref[:, lanes]
            out_ref[:, lanes] = (part + near).astype(out_ref.dtype)


def after(block, *others):
    return lax.optimization_barrier((block,) + others)[0]


def together(*blocks):
    return lax.optimization_barrier(blocks)


def sync(live):
    return dict(zip(live, together(*live.values())))


def per_device(queries, keys, values, kept_rows, out_weight):
    ctx, tp = lax.axis_index("ctx"), lax.axis_index("tp")
    x, z, core = ctx // 16, (ctx // 2) % NZ, ctx % 2

    col = jnp.arange(UNITS * DH)
    back = sum(jnp.where(col // DH == i, d, 0) for i, d in enumerate(ORDER))
    xs = ((x - jnp.arange(NX)) % NX).reshape(1, NX, 1, 1)
    block = xs * 16 + ((z - back) % NZ) * 2 + (core + col // KEEP) % 2
    asking = jnp.stack([ctx + 1 - 2 * core, ctx]).reshape(2, 1, 1, 1)
    seen = jnp.where(col // DH == UNITS - 1, asking > 0, (block >= 1) & (block < asking))
    flags = jnp.any(seen, (2, 3)).astype(jnp.int32)
    bias = jnp.where(seen, 0.0, MASKED).astype(F32)

    wide, kept = jax.ShapeDtypeStruct((BLK, 768), BF), jax.ShapeDtypeStruct((2, KEEP, DH), BF)
    quarters = jax.ShapeDtypeStruct((4, 2, DH, DH), BF)
    mine, send, kept, kept_send, first, first_send = call(
        prep_kernel,
        "prep",
        out_shape=(wide, wide, kept, kept, quarters, quarters),
        in_specs=[SMEM] + [VMEM] * 4,
        out_specs=(VMEM,) * 6,
    )(core.reshape(1), kept_rows.reshape(2, KEEP), queries, keys, values)
    live = dict(mine=mine, send=send, first=first, bias=bias)

    live["unit"] = jnp.concatenate([kept, to_core(kept_send)], 1)
    first = live["first"]
    first = jnp.where(ctx == 0, first, jnp.zeros_like(first))
    live["first"] = first + lax.ppermute(first_send, "ctx", [(0, 1)])
    live["weight"] = out_weight.T
    live = sync(live)

    unit, first = live["unit"], live["first"]
    live["up"], live["down"] = along_z(unit, 1), along_z(unit, -1)
    opposite = along_z(unit, 4)
    piece = first[0]
    for d in (1, 2, 3):
        pairs = [(ctx_id(0, 0, c), ctx_id(d, 0, c)) for c in range(2)]
        piece = piece + lax.ppermute(first[d], "ctx", pairs)
    live["piece"] = piece
    live["other"] = to_core(live.pop("send"))
    del live["first"]
    live = sync(live)

    def spread(piece, hop, starts):
        pairs = ctx_perm(lambda a, b, c: (a, b + hop, c), lambda a, b, c: b in starts)
        return lax.ppermute(piece, "ctx", pairs)

    unit, up, down, piece = live.pop("unit"), live.pop("up"), live.pop("down"), live.pop("piece")
    up2, down2 = together(jnp.stack([unit, up]), jnp.stack([unit, down]))
    up2, down2 = together(along_z(up2, 2), along_z(down2, -2))
    piece = piece + spread(piece, 4, (0,)) + spread(piece, 2, (0,)) + spread(piece, -2, (0,))
    piece = piece + spread(piece, 1, (0, 2, 4, 6))
    live["row"] = jnp.concatenate(
        [jnp.stack([unit, up]), up2, opposite[None], down2, jnp.stack([down, piece])]
    )
    live = sync(live)

    done = {}

    def ring_w(r):
        names = f"w{r - 1}", f"w{(NZ + 1 - r) % NZ}"
        up, down = live[names[0]], live[names[1]]
        for name in set(names):
            del live[name]
        if r == 4:
            up, down = together(up[:2], down[2:])
            done["w4u"], done["w4d"] = along_z(up, 1), along_z(down, -1)
        else:
            names = f"w{r}", f"w{NZ - r}"
            done[names[0]], done[names[1]] = along_z(up, 1), along_z(down, -1)
            live.update({name: done[name] for name in names})

    row = live["row"]
    live["left"], live["right"] = along_x(row, 1), along_x(row, -1)
    live["both"], live["acc"], live["tot"] = call(
        own_kernel,
        "own",
        1,
        out_shape=(jax.ShapeDtypeStruct((2, BLK, 768), BF), STATE, STATE),
        in_specs=[VMEM] * 2,
        out_specs=(VMEM,) * 3,
    )(live.pop("other"), live.pop("mine"))
    block_w = live.pop("weight")
    for k in range(4):
        pairs = [
            (ctx_id(a, b, c) * 4 + y, ctx_id(y - k, b, c) * 4 + a)
            for a in range(NX)
            for y in range(4)
            for b in range(NZ)
            for c in range(2)
        ]
        live[k] = lax.ppermute(block_w, ("ctx", "tp"), pairs)
    parts_w = jnp.stack([live.pop(k) for k in range(4)])
    mine_w = lax.dynamic_slice_in_dim(parts_w, core * 512, 512, 2)
    recv_w = to_core(lax.dynamic_slice_in_dim(parts_w, (1 - core) * 512, 512, 2))
    done["w0"] = live["w0"] = jnp.where(
        core == 0, jnp.concatenate([mine_w, recv_w], 1), jnp.concatenate([recv_w, mine_w], 1)
    )
    live["acc"], live["tot"] = call(
        functools.partial(both_kernel, 0),
        "step",
        2,
        out_shape=(STATE,) * 2,
        in_specs=[SMEM] + [VMEM] * 5,
        out_specs=(VMEM,) * 2,
        input_output_aliases={4: 0, 5: 1},
    )(flags, live["bias"], live["both"], row, live["acc"], live["tot"])
    live = sync(live)

    live["far_l"] = along_x(live["left"][:HEAD], 1)
    live["far_r"] = along_x(live["right"][HEAD:], -1)
    ring_w(1)
    behind = {name: live.pop(name) for name in ("w1", "w7")}
    half = jax.ShapeDtypeStruct(STATE.shape[1:], F32)
    near_parts = [(1, 0, UNITS), (3, 0, UNITS)]
    far_parts = [(2, 0, HEAD), (2, HEAD, UNITS)]
    live["acc0"], live["tot0"] = call(
        functools.partial(side_kernel, 0, near_parts),
        "step",
        2,
        out_shape=(half, half),
        in_specs=[SMEM] + [VMEM] * 6,
        out_specs=(VMEM,) * 2,
    )(flags, live["bias"], live["both"], live["acc"], live["tot"], live["left"], live["right"])
    live = sync(live)

    near, far = ("left", "right"), ("far_l", "far_r")

    def last(side, parts, states, pieces):
        names = ("row", "left", "far_l", "far_r", "right")
        return call(
            functools.partial(last_kernel, side, parts),
            "last",
            len(parts) / 2,
            vmem=20,
            out_shape=jax.ShapeDtypeStruct((BLK, 512), BF),
            in_specs=[SMEM] + [VMEM] * (4 + len(parts)) + [ANY] * 5,
            out_specs=VMEM,
            scratch_shapes=[
                pltpu.VMEM(STATE.shape[1:], F32),
                pltpu.VMEM(STATE.shape[1:], F32),
                pltpu.VMEM((NX, UNITS, 2, DH, DH), BF),
                pltpu.VMEM((BLK, 1), F32),
                pltpu.SemaphoreType.DMA((5,)),
            ],
        )(flags, live["bias"], live["both"], *[live[n] for n in states + pieces + names])

    live.update(behind)
    live["a0"] = last(0, far_parts, ("acc0", "tot0"), far)
    del live["acc0"], live["tot0"]
    live = sync(live)

    live["left0"], live["right0"] = over_tp(live["a0"], 1), over_tp(live["a0"], -1)
    ring_w(2)
    live["a1"] = last(1, near_parts + far_parts, ("acc", "tot"), near + far)
    for name in ("acc", "tot", "both", "bias", "row") + near + far:
        del live[name]
    live = sync(live)

    live["left1"], live["right1"] = over_tp(live["a1"], 1), over_tp(live["a1"], -1)
    ring_w(3)
    live = sync(live)

    far_l, far_r = together(
        jnp.stack([live["left0"][:, :256], live["left1"][:, :256]]),
        jnp.stack([live["right0"][:, 256:], live["right1"][:, 256:]]),
    )
    live["far_l"], live["far_r"] = over_tp(far_l, 1), over_tp(far_r, -1)
    ring_w(4)
    order = (0, 1, 7, 2, 6, 3, 5)
    where = [(tp + step - x) % 4 for step in (0, 3, 1, 2)] + [(z - d) % NZ for d in order + (4,)]
    where = jnp.stack(where).astype(jnp.int32)
    weights = [done[f"w{d}"] for d in order]

    def near_of(side):
        return [live[f"{name}{side}"] for name in ("a", "left", "right")]

    for side in (0, 1):
        live[f"near{side}"] = call(
            near_kernel,
            "near",
            1,
            vmem=16,
            out_shape=jax.ShapeDtypeStruct((BLK, 1024), F32),
            in_specs=[SMEM] + [VMEM] * 10,
            out_specs=VMEM,
        )(where, *near_of(side), *weights)
    live.update({name: done[name] for name in ("w4u", "w4d")})
    live = sync(live)

    def project(side, dtype):
        return call(
            functools.partial(far_kernel, side),
            "far",
            1,
            vmem=16,
            out_shape=jax.ShapeDtypeStruct((BLK, 1024), dtype),
            in_specs=[SMEM] + [VMEM] * 15,
            out_specs=VMEM,
        )(
            where, live[f"near{side}"], *near_of(side), live["far_l"], live["far_r"],
            *weights, live["w4u"], live["w4d"],
        )

    total = to_core(project(0, BF))
    return (project(1, F32) + total.astype(F32)).astype(BF)


def solution(mesh):
    placed = (P("ctx", "tp"), P("ctx", "tp"), P("ctx", "tp"), P("ctx", "tp", None), P("tp", "ctx"))
    return jax.shard_map(
        per_device, mesh=mesh, in_specs=placed, out_specs=P("ctx", "tp"), check_vma=False
    )
```

```python
import functools

import jax
import jax.numpy as jnp
import numpy as np
from jax import lax
from jax.experimental import pallas as pl
from jax.experimental.pallas import tpu as pltpu
from jax.sharding import PartitionSpec as P

DH = 128
BLK = 512
KEEP = 64
GROUP = 4
NX, NZ = 4, 8
ORDER = (0, 1, 2, 3, 4, 6, 5, 7)
UNITS, HEAD = 9, 5
SCALE = float(DH**-0.5 * np.log2(np.e))
MASKED = -1e30
LOW, HIGH = 1e-20, 1e30
BF, F32 = jnp.bfloat16, jnp.float32
VMEM = pl.BlockSpec(memory_space=pltpu.VMEM)
SMEM = pl.BlockSpec(memory_space=pltpu.SMEM)
ANY = pl.BlockSpec(memory_space=pl.ANY)
HBM = pl.BlockSpec(memory_space=pltpu.HBM)
STATE = jax.ShapeDtypeStruct((2, GROUP, BLK, DH), F32)
NT = (((1,), (1,)), ((), ()))


def ctx_id(x, z, core):
    return (x % NX) * 16 + (z % NZ) * 2 + core % 2


def ctx_perm(move, keep=lambda x, z, core: True):
    places = [(x, z, core) for x in range(NX) for z in range(NZ) for core in range(2)]
    return [(ctx_id(*at), ctx_id(*move(*at))) for at in places if keep(*at)]


def along_x(block, step):
    return lax.ppermute(block, "ctx", ctx_perm(lambda x, z, core: (x + step, z, core)))


def along_z(block, step):
    return lax.ppermute(block, "ctx", ctx_perm(lambda x, z, core: (x, z + step, core)))


def to_core(block):
    return lax.ppermute(block, "ctx", ctx_perm(lambda x, z, core: (x, z, core + 1)))


def over_tp(block, step):
    return lax.ppermute(block, "tp", [(y, (y + step) % 4) for y in range(4)])


def call(kernel, name, pieces=0, vmem=12, **kw):
    cost = pl.CostEstimate(flops=int(5e8 + 2.4e9 * pieces), bytes_accessed=2**20, transcendentals=0)
    params = pltpu.CompilerParams(vmem_limit_bytes=vmem * 2**20)
    return pl.pallas_call(kernel, name=name, cost_estimate=cost, compiler_params=params, **kw)


def prep_kernel(core_ref, rows_ref, k_ref, v_ref, *refs):
    mine_ref, send_ref, kept_ref, kept_send_ref, first_ref, first_send_ref = refs
    row = lax.broadcasted_iota(jnp.int32, (BLK, KEEP), 0)
    core = core_ref[0]
    for head, out, kept, first in (
        (core, mine_ref, kept_ref, first_ref),
        (1 - core, send_ref, kept_send_ref, first_send_ref),
    ):
        lanes = pl.ds(pl.multiple_of(head * DH, DH), DH)
        pick = jnp.where(rows_ref[pl.ds(head, 1), :] == row, 1.0, 0.0).astype(BF)
        for at, ref in enumerate((k_ref, v_ref)):
            block = ref[:, lanes]
            kept[at] = lax.dot_general(
                pick, block, (((0,), (0,)), ((), ())), preferred_element_type=F32
            ).astype(BF)
            out[:, at * DH : at * DH + DH] = block
            for quarter in range(4):
                first[quarter, at] = block[quarter * DH : (quarter + 1) * DH]


def join_kernel(core_ref, q_ref, mine_kv, send_kv, mine_ref, send_ref):
    core = core_ref[0]
    for head, kv, out in ((core, mine_kv, mine_ref), (1 - core, send_kv, send_ref)):
        out[:, :512] = q_ref[:, pl.ds(pl.multiple_of(head * 512, 512), 512)]
        out[:, 512:] = kv[...]


def scores_of(q, k):
    return lax.dot_general(q, k, NT, preferred_element_type=F32) * SCALE


def lane_sum(p):
    total = p[:, :DH]
    for at in range(DH, p.shape[1], DH):
        total = total + p[:, at : at + DH]
    return total


def group_lanes(g):
    return slice(g * DH, (g + 1) * DH)


def causal(s, first=0):
    row = first + lax.broadcasted_iota(jnp.int32, s.shape, 0)
    col = lax.broadcasted_iota(jnp.int32, s.shape, 1)
    return jnp.where(row >= col, s, MASKED)


def own_kernel(other_ref, mine_ref, q_ref, acc, tot):
    q_ref[0] = other_ref[...]
    q_ref[1] = mine_ref[...]

    def side_step(side, carry):
        for g in range(GROUP):
            for first in (0, 256):
                rows, upto = slice(first, first + 256), first + 256
                s = scores_of(q_ref[side, rows, group_lanes(g)], q_ref[side, :upto, 512:640])
                p = jnp.exp2(causal(s, first))
                tot[side, g, rows] = lane_sum(p)
                acc[side, g, rows] = jnp.dot(
                    p.astype(BF), q_ref[side, :upto, 640:], preferred_element_type=F32
                )
        return carry

    lax.fori_loop(0, 2, side_step, 0)


def keys_of(piece):
    rows = piece.shape[0] * DH
    return piece[:, 0].reshape(rows, DH), piece[:, 1].reshape(rows, DH)


def absorb(q_ref, piece_ref, flag, bias, acc, tot):
    @pl.when(flag > 0)
    def _():
        k, v = keys_of(piece_ref)
        for g in range(GROUP):
            p = jnp.exp2(scores_of(q_ref[:, group_lanes(g)], k) + bias)
            tot[g] += lane_sum(p)
            acc[g] += jnp.dot(p.astype(BF), v, preferred_element_type=F32)


def both_kernel(at, flag_ref, bias_ref, q_ref, piece, _acc, _tot, acc, tot):
    def side_step(side, carry):
        absorb(q_ref.at[side], piece, flag_ref[side, at], bias_ref[side, at], acc.at[side], tot.at[side])
        return carry

    lax.fori_loop(0, 2, side_step, 0)


def absorb_all(side, parts, flag_ref, bias_ref, q_ref, pieces, acc, tot):
    for (at, lo, hi), piece in zip(parts, pieces):
        bias = bias_ref[side, at, :, lo * DH : hi * DH]
        absorb(q_ref, piece, flag_ref[side, at], bias, acc, tot)


def side_kernel(side, parts, flag_ref, bias_ref, both_ref, acc_in, tot_in, *refs):
    pieces, (acc, tot) = refs[: len(parts)], refs[len(parts) :]
    acc[...] = acc_in[side]
    tot[...] = tot_in[side]
    absorb_all(side, parts, flag_ref, bias_ref, both_ref.at[side], pieces, acc, tot)


def last_kernel(side, parts, flag_ref, bias_ref, both_ref, acc_in, tot_in, *refs):
    pieces, refs = refs[: len(parts)], refs[len(parts) :]
    everything, (out_ref, acc, tot, kv, top, sems) = refs[:5], refs[5:]
    q_ref = both_ref.at[side]
    acc[...] = acc_in[side] if len(acc_in.shape) == 4 else acc_in[...]
    tot[...] = tot_in[side] if len(tot_in.shape) == 4 else tot_in[...]
    absorb_all(side, parts, flag_ref, bias_ref, q_ref, pieces, acc, tot)
    sums = [jnp.sum(tot[g], 1, keepdims=True) for g in range(GROUP)]
    least = jnp.min(functools.reduce(jnp.minimum, sums))
    most = jnp.max(functools.reduce(jnp.maximum, sums))

    @pl.when(jnp.logical_not((least > LOW) & (most < HIGH)))
    def _():
        places = [kv.at[0], kv.at[1], kv.at[2, :HEAD], kv.at[2, HEAD:], kv.at[3]]
        copies = [
            pltpu.make_async_copy(ref, place, sems.at[i])
            for i, (ref, place) in enumerate(zip(everything, places))
        ]
        for copy in copies:
            copy.start()
        for copy in copies:
            copy.wait()

        def one_group(g, carry):
            q = q_ref[:, pl.ds(pl.multiple_of(g * DH, DH), DH)]
            s = causal(scores_of(q, q_ref[:, 512:640]))
            peak = jnp.max(s, 1, keepdims=True)
            p = jnp.exp2(s - peak)
            top[...] = peak
            tot[g] = lane_sum(p)
            acc[g] = jnp.dot(p.astype(BF), q_ref[:, 640:], preferred_element_type=F32)

            def one_piece(i, carry):
                @pl.when(flag_ref[side, i] > 0)
                def _():
                    k, v = keys_of(kv.at[i])
                    s = scores_of(q, k) + bias_ref[side, i]
                    old = top[...]
                    peak = jnp.maximum(old, jnp.max(s, 1, keepdims=True))
                    fade = jnp.exp2(old - peak)
                    p = jnp.exp2(s - peak)
                    top[...] = peak
                    tot[g] = tot[g] * fade + lane_sum(p)
                    acc[g] = acc[g] * fade + jnp.dot(p.astype(BF), v, preferred_element_type=F32)

                return carry

            return lax.fori_loop(0, NX, one_piece, carry)

        lax.fori_loop(0, GROUP, one_group, 0)

    for g in range(GROUP):
        total = jnp.sum(tot[g], 1, keepdims=True)
        out_ref[:, group_lanes(g)] = (acc[g] / total).astype(BF)


def products(blocks, weights, where_ref, slots, group):
    total = None
    for block, (slot, lo, hi) in zip(blocks, slots):
        k = where_ref[slot]
        w = jnp.concatenate([weights[i](k, lo, hi) for i in group])
        term = lax.dot_general(block, w, NT, preferred_element_type=F32)
        total = term if total is None else total + term
    return [total[:, i * DH : (i + 1) * DH] for i in range(len(group))]


def lanes_of(where_ref, i):
    return pl.ds(pl.multiple_of(where_ref[4 + i] * DH, DH), DH)


def piece_of(ref):
    return lambda k, lo, hi: ref[k, :, lo:hi]


NEAR = ((0, 0, 512), (1, 0, 512), (2, 0, 512))
FAR = ((3, 0, 256), (3, 256, 512))


def near_kernel(where_ref, *refs):
    blocks, weights, out_ref = refs[:3], [piece_of(ref) for ref in refs[3:10]], refs[10]
    for group in ((0, 1), (2, 3), (4, 5), (6,)):
        parts = products([ref[...] for ref in blocks], weights, where_ref, NEAR, group)
        for i, part in zip(group, parts):
            out_ref[:, lanes_of(where_ref, i)] = part


def far_kernel(side, where_ref, near_ref, *refs):
    blocks, far, weights, (up, down, out_ref) = refs[:3], refs[3:5], refs[5:12], refs[12:]

    def last_piece(k, lo, hi):
        return jnp.where(k < 2, up[jnp.minimum(k, 1), :, lo:hi], down[jnp.maximum(k - 2, 0), :, lo:hi])

    weights = [piece_of(ref) for ref in weights] + [last_piece]
    for group in ((0, 1), (2, 3), (4, 5), (6, 7)):
        parts = products([ref[side] for ref in far], weights, where_ref, FAR, group)
        for i, part in zip(group, parts):
            lanes = lanes_of(where_ref, i)
            if i == 7:
                near = products([ref[...] for ref in blocks], weights, where_ref, NEAR, (7,))[0]
            else:
                near = near_ref[:, lanes]
            out_ref[:, lanes] = (part + near).astype(out_ref.dtype)


def after(block, *others):
    return lax.optimization_barrier((block,) + others)[0]


def together(*blocks):
    return lax.optimization_barrier(blocks)


def sync(live):
    return dict(zip(live, together(*live.values())))


def per_device(queries, keys, values, kept_rows, out_weight):
    ctx, tp = lax.axis_index("ctx"), lax.axis_index("tp")
    x, z, core = ctx // 16, (ctx // 2) % NZ, ctx % 2

    col = jnp.arange(UNITS * DH)
    back = sum(jnp.where(col // DH == i, d, 0) for i, d in enumerate(ORDER))
    xs = ((x - jnp.arange(NX)) % NX).reshape(1, NX, 1, 1)
    block = xs * 16 + ((z - back) % NZ) * 2 + (core + col // KEEP) % 2
    asking = jnp.stack([ctx + 1 - 2 * core, ctx]).reshape(2, 1, 1, 1)
    seen = jnp.where(col // DH == UNITS - 1, asking > 0, (block >= 1) & (block < asking))
    flags = jnp.any(seen, (2, 3)).astype(jnp.int32)
    bias = jnp.where(seen, 0.0, MASKED).astype(F32)

    wide, kept = jax.ShapeDtypeStruct((BLK, 768), BF), jax.ShapeDtypeStruct((2, KEEP, DH), BF)
    quarters = jax.ShapeDtypeStruct((4, 2, DH, DH), BF)
    narrow = jax.ShapeDtypeStruct((BLK, 2 * DH), BF)
    place = core.reshape(1)
    mine_kv, send_kv, kept, kept_send, first, first_send = call(
        prep_kernel,
        "prep",
        out_shape=(narrow, narrow, kept, kept, quarters, quarters),
        in_specs=[SMEM] + [VMEM] * 3,
        out_specs=(VMEM,) * 6,
    )(place, kept_rows.reshape(2, KEEP), keys, values)
    live = dict(first=first, bias=bias)

    live["unit"] = jnp.concatenate([kept, to_core(kept_send)], 1)
    first = live["first"]
    first = jnp.where(ctx == 0, first, jnp.zeros_like(first))
    live["first"] = first + lax.ppermute(first_send, "ctx", [(0, 1)])
    live["weight"] = out_weight.T
    live = sync(live)

    unit, first = live["unit"], live["first"]
    live["up"], live["down"] = along_z(unit, 1), along_z(unit, -1)
    opposite = along_z(unit, 4)
    piece = first[0]
    for d in (1, 2, 3):
        pairs = [(ctx_id(0, 0, c), ctx_id(d, 0, c)) for c in range(2)]
        piece = piece + lax.ppermute(first[d], "ctx", pairs)
    live["piece"] = piece
    live["mine"], send = call(
        join_kernel,
        "join",
        out_shape=(wide, wide),
        in_specs=[SMEM] + [VMEM] * 3,
        out_specs=(VMEM,) * 2,
    )(place, queries, mine_kv, send_kv)
    live["other"] = to_core(send)
    del live["first"]
    live = sync(live)

    def spread(piece, hop, starts):
        pairs = ctx_perm(lambda a, b, c: (a, b + hop, c), lambda a, b, c: b in starts)
        return lax.ppermute(piece, "ctx", pairs)

    unit, up, down, piece = live.pop("unit"), live.pop("up"), live.pop("down"), live.pop("piece")
    up2, down2 = together(jnp.stack([unit, up]), jnp.stack([unit, down]))
    up2, down2 = together(along_z(up2, 2), along_z(down2, -2))
    piece = piece + spread(piece, 4, (0,)) + spread(piece, 2, (0,)) + spread(piece, -2, (0,))
    piece = piece + spread(piece, 1, (0, 2, 4, 6))
    live["row"] = jnp.concatenate(
        [jnp.stack([unit, up]), up2, opposite[None], down2, jnp.stack([down, piece])]
    )
    live = sync(live)

    done = {}

    def ring_w(r, *ties):
        names = f"w{r - 1}", f"w{(NZ + 1 - r) % NZ}"
        up, down = live[names[0]], live[names[1]]
        for name in set(names):
            del live[name]
        if r == 4:
            up, down = together(up[:2], down[2:], *ties)[:2]
            done["w4u"], done["w4d"] = along_z(up, 1), along_z(down, -1)
        else:
            names = f"w{r}", f"w{NZ - r}"
            done[names[0]], done[names[1]] = along_z(up, 1), along_z(down, -1)
            live.update({name: done[name] for name in names})

    row = live["row"]
    live["left"], live["right"] = along_x(row, 1), along_x(row, -1)
    live["both"], live["acc"], live["tot"] = call(
        own_kernel,
        "own",
        1,
        out_shape=(jax.ShapeDtypeStruct((2, BLK, 768), BF), STATE, STATE),
        in_specs=[VMEM] * 2,
        out_specs=(VMEM,) * 3,
    )(live.pop("other"), live.pop("mine"))
    block_w = live.pop("weight")
    for k in range(4):
        pairs = [
            (ctx_id(a, b, c) * 4 + y, ctx_id(y - k, b, c) * 4 + a)
            for a in range(NX)
            for y in range(4)
            for b in range(NZ)
            for c in range(2)
        ]
        block = after(block_w, live["acc"]) if k == 3 else block_w
        live[k] = lax.ppermute(block, ("ctx", "tp"), pairs)
    parts_w = jnp.stack([live.pop(k) for k in range(4)])
    mine_w = lax.dynamic_slice_in_dim(parts_w, core * 512, 512, 2)
    recv_w = to_core(lax.dynamic_slice_in_dim(parts_w, (1 - core) * 512, 512, 2))
    done["w0"] = live["w0"] = jnp.where(
        core == 0, jnp.concatenate([mine_w, recv_w], 1), jnp.concatenate([recv_w, mine_w], 1)
    )
    live["acc"], live["tot"] = call(
        functools.partial(both_kernel, 0),
        "step",
        2,
        out_shape=(STATE,) * 2,
        in_specs=[SMEM] + [VMEM] * 5,
        out_specs=(VMEM,) * 2,
        input_output_aliases={4: 0, 5: 1},
    )(flags, live["bias"], live["both"], row, live["acc"], live["tot"])
    live = sync(live)

    live["far_l"] = along_x(live["left"][:HEAD], 1)
    live["far_r"] = along_x(live["right"][HEAD:], -1)
    ring_w(1)
    behind = {name: live.pop(name) for name in ("w1", "w7")}
    half = jax.ShapeDtypeStruct(STATE.shape[1:], F32)
    near_parts = [(1, 0, UNITS), (3, 0, UNITS)]
    far_parts = [(2, 0, HEAD), (2, HEAD, UNITS)]
    live["acc0"], live["tot0"] = call(
        functools.partial(side_kernel, 0, near_parts),
        "step",
        2,
        out_shape=(half, half),
        in_specs=[SMEM] + [VMEM] * 6,
        out_specs=(VMEM,) * 2,
    )(flags, live["bias"], live["both"], live["acc"], live["tot"], live["left"], live["right"])
    live = sync(live)

    near, far = ("left", "right"), ("far_l", "far_r")

    def last(side, parts, states, pieces):
        names = ("row", "left", "far_l", "far_r", "right")
        return call(
            functools.partial(last_kernel, side, parts),
            "last",
            len(parts) / 2,
            vmem=20,
            out_shape=jax.ShapeDtypeStruct((BLK, 512), BF),
            in_specs=[SMEM] + [VMEM] * (4 + len(parts)) + [ANY] * 5,
            out_specs=VMEM,
            scratch_shapes=[
                pltpu.VMEM(STATE.shape[1:], F32),
                pltpu.VMEM(STATE.shape[1:], F32),
                pltpu.VMEM((NX, UNITS, 2, DH, DH), BF),
                pltpu.VMEM((BLK, 1), F32),
                pltpu.SemaphoreType.DMA((5,)),
            ],
        )(flags, live["bias"], live["both"], *[live[n] for n in states + pieces + names])

    live.update(behind)
    live["a0"] = last(0, far_parts, ("acc0", "tot0"), far)
    del live["acc0"], live["tot0"]
    live = sync(live)

    live["left0"], live["right0"] = over_tp(live["a0"], 1), over_tp(live["a0"], -1)
    ring_w(2)
    live["a1"] = last(1, near_parts + far_parts, ("acc", "tot"), near + far)
    for name in ("acc", "tot", "both", "bias", "row") + near + far:
        del live[name]
    live = sync(live)

    live["left1"], live["right1"] = over_tp(live["a1"], 1), over_tp(live["a1"], -1)
    ring_w(3)
    live = sync(live)

    far_l, far_r = together(
        jnp.stack([live["left0"][:, :256], live["left1"][:, :256]]),
        jnp.stack([live["right0"][:, 256:], live["right1"][:, 256:]]),
    )
    live["far_l"], live["far_r"] = over_tp(far_l, 1), over_tp(far_r, -1)
    ring_w(4, far_l, far_r)
    order = (0, 1, 7, 2, 6, 3, 5)
    where = [(tp + step - x) % 4 for step in (0, 3, 1, 2)] + [(z - d) % NZ for d in order + (4,)]
    where = jnp.stack(where).astype(jnp.int32)
    weights = [done[f"w{d}"] for d in order]

    def near_of(side):
        return [live[f"{name}{side}"] for name in ("a", "left", "right")]

    for side in (0, 1):
        live[f"near{side}"] = call(
            near_kernel,
            "near",
            1,
            vmem=16,
            out_shape=jax.ShapeDtypeStruct((BLK, 1024), F32),
            in_specs=[SMEM] + [VMEM] * 10,
            out_specs=VMEM,
        )(where, *near_of(side), *weights)
    live.update({name: done[name] for name in ("w4u", "w4d")})
    live = sync(live)

    def project(side, dtype):
        return call(
            functools.partial(far_kernel, side),
            "far",
            1,
            vmem=16,
            out_shape=jax.ShapeDtypeStruct((BLK, 1024), dtype),
            in_specs=[SMEM] + [VMEM] * 15,
            out_specs=VMEM,
        )(
            where, live[f"near{side}"], *near_of(side), live["far_l"], live["far_r"],
            *weights, live["w4u"], live["w4d"],
        )

    total = to_core(project(0, BF))
    return (project(1, F32) + total.astype(F32)).astype(BF)


def solution(mesh):
    placed = (P("ctx", "tp"), P("ctx", "tp"), P("ctx", "tp"), P("ctx", "tp", None), P("tp", "ctx"))
    return jax.shard_map(
        per_device, mesh=mesh, in_specs=placed, out_specs=P("ctx", "tp"), check_vma=False
    )
```
